32 devices in a mesh: jobs: 2 (over y), fsdp: 8 (over z, x), grp: 2 (over core).
Axes of the slice: x: 2, y: 2, z: 4, core: 2. Of those that a mesh axis runs over, the one named last changes fastest.
Arguments:
- tokens: bfloat16 [1024, 8192], P(('jobs', 'grp'), 'fsdp'), parts along dimension 0, may hold values from -6 to 6
- cotangent: bfloat16 [1024, 8192], P(('jobs', 'grp'), 'fsdp'), parts along dimension 0, may hold values from -6 to 6
- w_gate: bfloat16 [8192, 16384], P('grp', 'fsdp'), may hold values from -0.0625 to 0.0625
- w_up: bfloat16 [8192, 16384], P('grp', 'fsdp'), may hold values from -0.0625 to 0.0625
- w_down: bfloat16 [16384, 8192], P('fsdp', 'grp'), may hold values from -0.046875 to 0.046875
- adapt_model: bfloat16 [6, 16, 8192], P('jobs', None, 'fsdp'), parts along dimension 0, may hold values from -0.0625 to 0.0625
- adapt_hidden: bfloat16 [6, 16, 16384], P('jobs', None, 'fsdp'), parts along dimension 0, may hold values from -0.19921875 to 0.19921875
- direction_model: float32 [6, 16, 8192], P('jobs', None, 'fsdp'), parts along dimension 0, may hold values from -60 to 60
- direction_hidden: float32 [6, 16, 16384], P('jobs', None, 'fsdp'), parts along dimension 0, may hold values from -60 to 60
- previous_model: float32 [6, 16, 8192], P('jobs', None, 'fsdp'), parts along dimension 0, may hold values from -6 to 6
- previous_hidden: float32 [6, 16, 16384], P('jobs', None, 'fsdp'), parts along dimension 0, may hold values from -6 to 6
- beta_prev: float32 [2], P('jobs'), parts along dimension 0, may hold values from 1000 to 10000
Outputs:
- next_model: float32 [6, 16, 8192], P('jobs', None, 'fsdp'), parts along dimension 0
- next_hidden: float32 [6, 16, 16384], P('jobs', None, 'fsdp'), parts along dimension 0
- alpha_out: float32 [2], P('jobs'), parts along dimension 0
The draws below stay inside these ranges and needn't reach their ends.
There are 2 independent parts, one for each index of `jobs`. The reference program is written for one: setup_inputs(seed, part) draws one part's arguments, and reference() takes and returns one part's arrays. A program takes and returns all parts, laid end to end along the dimension named above; an argument that names none is the same for every part. Nothing has to cross between parts.
All inputs are finite; a program needn't handle non-finite values.
Results may differ from the reference program's by a relative error of at most 0.0029.
Values may be sent and summed in bfloat16 or wider, within the bound.
A program may use at most 320 MiB of HBM per device.

```python
import math
import jax
import jax.numpy as jnp
from jax import lax

D = 8192
FF = 16384
R = 16
TOKENS = 512


def ramp_draw(key, width, rise):
    values = jnp.clip(jax.random.normal(key, (3, R, width), jnp.float32), -6.0, 6.0)
    place = jnp.arange(width, dtype=jnp.float32) / width
    return values * jnp.exp(jnp.log(rise) * place)[None, None, :]


def draw_direction_model(key, part):
    key = jax.random.fold_in(key, 11)
    return ramp_draw(key, D, 3.0)


def draw_direction_hidden(key, part):
    key = jax.random.fold_in(key, 23)
    return ramp_draw(key, FF, 3.0)


def block_levels(rng, dims, split, least, high):
    factor_of, own = 1.0, jax.random.fold_in(rng, 6)
    for position, parts in split:
        steps = jnp.exp(jax.random.uniform(jax.random.fold_in(own, position), (parts,), jnp.float32, least / len(split), high / len(split)))
        factor_of = factor_of * jnp.repeat(steps, dims[position] // parts).reshape([-1 if axis == position else 1 for axis in range(len(dims))])
    return factor_of


def normal_values(key, extent, scale, bound, shards=(), kind=jnp.bfloat16):
    result = jax.random.normal(key, extent, jnp.float32) * scale
    if len(shards) > 0:
        result = block_levels(key, extent, shards, -0.22, 0.18) * result
    return jnp.clip(result, min=-bound, max=bound).astype(kind)


def setup_inputs(seed: int = 0, part: int = 0) -> dict:
    splits = jax.random.split(jax.random.key(seed), 13)
    part_keys = jax.random.split(jax.random.fold_in(splits[12], part), 13)
    return {
        "tokens": normal_values(part_keys[0], (TOKENS, D), 1.0, 6.0, ((0, 2), (1, 8))),
        "cotangent": normal_values(part_keys[1], (TOKENS, D), 1.0, 6.0, ((0, 2), (1, 8))),
        "w_gate": normal_values(splits[2], (D, FF), D ** -0.5, 0.0625, ((0, 2), (1, 8))),
        "w_up": normal_values(splits[3], (D, FF), D ** -0.5, 0.0625, ((0, 2), (1, 8))),
        "w_down": normal_values(splits[4], (FF, D), FF ** -0.5, 0.046875, ((0, 8), (1, 2))),
        "adapt_model": normal_values(part_keys[5], (3, R, D), D ** -0.5, 0.0625, ((2, 8),)),
        "adapt_hidden": normal_values(part_keys[6], (3, R, FF), 0.03, 0.19921875, ((2, 8),)),
        "direction_model": draw_direction_model(jax.random.fold_in(jax.random.fold_in(splits[12], part), 71), part),
        "direction_hidden": draw_direction_hidden(jax.random.fold_in(jax.random.fold_in(splits[12], part), 71), part),
        "previous_model": normal_values(part_keys[9], (3, R, D), 1.0, 6.0, ((2, 8),), jnp.float32),
        "previous_hidden": normal_values(part_keys[10], (3, R, FF), 1.0, 6.0, ((2, 8),), jnp.float32),
        "beta_prev": jnp.clip(jnp.exp(jax.random.uniform(part_keys[11], (1,), jnp.float32, math.log(1000.0), math.log(10000.0))), 1000.0, 10000.0),
    }


adapter_scale = 2.0

def gated_product(left, right):
    return jnp.dot(left, right, precision=lax.Precision.HIGHEST, preferred_element_type=jnp.float32)

def reference(tokens, cotangent, w_gate, w_up, w_down, adapt_model, adapt_hidden, direction_model, direction_hidden, previous_model, previous_hidden, beta_prev):
    dir_model = direction_model.astype(jnp.bfloat16).astype(jnp.float32)
    dir_hidden = direction_hidden.astype(jnp.bfloat16).astype(jnp.float32)
    gate_baseline = jnp.dot(tokens, w_gate, preferred_element_type=jnp.float32)
    up_baseline = jnp.dot(tokens, w_up, preferred_element_type=jnp.float32)
    backward_baseline = jnp.dot(cotangent, w_down.T, preferred_element_type=jnp.float32)
    tokens_gathered = tokens.astype(jnp.float32)
    cotangent_gathered = cotangent.astype(jnp.float32)
    low_model = adapt_model.astype(jnp.float32)
    reduced_hidden = adapt_hidden.astype(jnp.float32)
    projected_gate = gated_product(low_model[0], tokens_gathered.T)
    projected_up = gated_product(low_model[1], tokens_gathered.T)
    projected_cotangent = gated_product(low_model[2], cotangent_gathered.T)
    tangent_projected_gate = gated_product(dir_model[0], tokens_gathered.T)
    tangent_projected_up = gated_product(dir_model[1], tokens_gathered.T)
    tangent_projected_cotangent = gated_product(dir_model[2], cotangent_gathered.T)
    adapter_gate_factor, adapter_up_factor, adapter_down_factor = (reduced_hidden[0], reduced_hidden[1], reduced_hidden[2])
    direction_gate_adapter, direction_up_adapter, direction_down_adapter = (dir_hidden[0], dir_hidden[1], dir_hidden[2])
    gate_preactivation = gate_baseline + adapter_scale * gated_product(projected_gate.T, adapter_gate_factor)
    up_preactivation = up_baseline + adapter_scale * gated_product(projected_up.T, adapter_up_factor)
    tangent_gate = adapter_scale * (gated_product(tangent_projected_gate.T, adapter_gate_factor) + gated_product(projected_gate.T, direction_gate_adapter))
    tangent_up = adapter_scale * (gated_product(tangent_projected_up.T, adapter_up_factor) + gated_product(projected_up.T, direction_up_adapter))
    sig_gate = jax.nn.sigmoid(gate_preactivation)
    act_gate = gate_preactivation * sig_gate
    slope_one = sig_gate * (1.0 + gate_preactivation * (1.0 - sig_gate))
    slope_two = sig_gate * (1.0 - sig_gate) * (2.0 + gate_preactivation * (1.0 - 2.0 * sig_gate))
    hidden_state = act_gate * up_preactivation
    tangent_hidden = slope_one * tangent_gate * up_preactivation + act_gate * tangent_up
    hidden_gradient = backward_baseline + adapter_scale * gated_product(projected_cotangent.T, adapter_down_factor)
    tangent_hidden_gradient = adapter_scale * (gated_product(tangent_projected_cotangent.T, adapter_down_factor) + gated_product(projected_cotangent.T, direction_down_adapter))
    gate_gradient = hidden_gradient * up_preactivation * slope_one
    up_gradient = hidden_gradient * act_gate
    tangent_gate_gradient = tangent_hidden_gradient * up_preactivation * slope_one + hidden_gradient * tangent_up * slope_one + hidden_gradient * up_preactivation * slope_two * tangent_gate
    tangent_up_gradient = tangent_hidden_gradient * act_gate + hidden_gradient * slope_one * tangent_gate
    blended_gate = adapter_scale * (gated_product(direction_gate_adapter, gate_gradient.T) + gated_product(adapter_gate_factor, tangent_gate_gradient.T))
    blended_up = adapter_scale * (gated_product(direction_up_adapter, up_gradient.T) + gated_product(adapter_up_factor, tangent_up_gradient.T))
    tangent_reduced_down = gated_product(adapter_down_factor, tangent_hidden.T) + gated_product(direction_down_adapter, hidden_state.T)
    curvature_model = jnp.stack([gated_product(blended_gate, tokens_gathered), gated_product(blended_up, tokens_gathered), adapter_scale * gated_product(tangent_reduced_down, cotangent_gathered)])
    curvature_hidden = jnp.stack([adapter_scale * (gated_product(tangent_projected_gate, gate_gradient) + gated_product(projected_gate, tangent_gate_gradient)), adapter_scale * (gated_product(tangent_projected_up, up_gradient) + gated_product(projected_up, tangent_up_gradient)), adapter_scale * (gated_product(tangent_projected_cotangent, hidden_state) + gated_product(projected_cotangent, tangent_hidden))])
    along = jnp.sum(curvature_model * direction_model) + jnp.sum(curvature_hidden * direction_hidden)
    square = jnp.sum(direction_model * direction_model) + jnp.sum(direction_hidden * direction_hidden)
    alpha = along / square
    beta = beta_prev[0]
    resid_model = curvature_model - alpha * direction_model - beta * previous_model
    resid_hidden = curvature_hidden - alpha * direction_hidden - beta * previous_hidden
    total = jnp.sum(resid_model * resid_model) + jnp.sum(resid_hidden * resid_hidden)
    factor = lax.rsqrt(total / (R * (3 * D + 3 * FF)) + 1e-06)
    return (resid_model * factor, resid_hidden * factor, jnp.reshape(alpha, (1,)))
```

```python
import functools
import jax
import jax.numpy as jnp
from jax import lax
from jax.experimental import pallas as pl
from jax.experimental.pallas import tpu as pltpu
from jax.sharding import PartitionSpec as P

D = 8192
FF = 16384
R = 16


adapter_scale = 2.0


def gated_product(left, right):
    return jnp.dot(left, right, precision=lax.Precision.HIGHEST, preferred_element_type=jnp.float32)


def lowrank_terms(adapt_part, dir_part, tok_part, cot_part):
    left_tok = jnp.concatenate([adapt_part[:2], dir_part[:2]], 0)
    left_cot = jnp.stack([adapt_part[2], dir_part[2]])
    low_tok = jnp.einsum("krn,tn->krt", left_tok, tok_part, preferred_element_type=jnp.float32)
    low_cot = jnp.einsum("krn,tn->krt", left_cot, cot_part, preferred_element_type=jnp.float32)
    return (low_tok, low_cot)


def body(
    tokens,
    cotangent,
    w_gate,
    w_up,
    w_down,
    adapt_model,
    adapt_hidden,
    direction_model,
    direction_hidden,
    previous_model,
    previous_hidden,
    beta_prev,
):
    dir_model = direction_model.astype(jnp.bfloat16)
    dir_hidden = direction_hidden.astype(jnp.bfloat16)
    full_gate, full_up = (
        lax.all_gather(w_gate, "grp", axis=0, tiled=True),
        lax.all_gather(w_up, "grp", axis=0, tiled=True),
    )
    full_down = lax.all_gather(w_down, "grp", axis=1, tiled=True)
    wide_adapt, wide_dir = (
        lax.all_gather(adapt_model, "fsdp", axis=2, tiled=True),
        lax.all_gather(dir_model, "fsdp", axis=2, tiled=True),
    )
    tok_full, cot_full = (
        lax.all_gather(tokens, "fsdp", axis=1, tiled=True),
        lax.all_gather(cotangent, "fsdp", axis=1, tiled=True),
    )
    gate_baseline = jnp.dot(tok_full, full_gate, preferred_element_type=jnp.float32)
    up_baseline = jnp.dot(tok_full, full_up, preferred_element_type=jnp.float32)
    backward_baseline = lax.dot_general(
        cot_full, full_down, (((1,), (1,)), ((), ())), preferred_element_type=jnp.float32
    )
    low_tok, low_cot = lowrank_terms(wide_adapt, wide_dir, tok_full, cot_full)
    projected_gate, projected_up, tangent_projected_gate, tangent_projected_up = (
        low_tok[0],
        low_tok[1],
        low_tok[2],
        low_tok[3],
    )
    projected_cotangent, tangent_projected_cotangent = (low_cot[0], low_cot[1])
    reduced_hidden = adapt_hidden.astype(jnp.float32)
    tan_hidden_dir = dir_hidden.astype(jnp.float32)
    adapter_gate_factor, adapter_up_factor, adapter_down_factor = (
        reduced_hidden[0],
        reduced_hidden[1],
        reduced_hidden[2],
    )
    direction_gate_adapter, direction_up_adapter, direction_down_adapter = (
        tan_hidden_dir[0],
        tan_hidden_dir[1],
        tan_hidden_dir[2],
    )
    gate_preactivation = gate_baseline + adapter_scale * gated_product(
        projected_gate.T, adapter_gate_factor
    )
    up_preactivation = up_baseline + adapter_scale * gated_product(
        projected_up.T, adapter_up_factor
    )
    tangent_gate = adapter_scale * (
        gated_product(tangent_projected_gate.T, adapter_gate_factor)
        + gated_product(projected_gate.T, direction_gate_adapter)
    )
    tangent_up = adapter_scale * (
        gated_product(tangent_projected_up.T, adapter_up_factor)
        + gated_product(projected_up.T, direction_up_adapter)
    )
    sig_gate = jax.nn.sigmoid(gate_preactivation)
    act_gate = gate_preactivation * sig_gate
    slope_one = sig_gate * (1.0 + gate_preactivation * (1.0 - sig_gate))
    slope_two = sig_gate * (1.0 - sig_gate) * (2.0 + gate_preactivation * (1.0 - 2.0 * sig_gate))
    hidden_state = act_gate * up_preactivation
    tangent_hidden = slope_one * tangent_gate * up_preactivation + act_gate * tangent_up
    hidden_gradient = backward_baseline + adapter_scale * gated_product(
        projected_cotangent.T, adapter_down_factor
    )
    tangent_hidden_gradient = adapter_scale * (
        gated_product(tangent_projected_cotangent.T, adapter_down_factor)
        + gated_product(projected_cotangent.T, direction_down_adapter)
    )
    gate_gradient = hidden_gradient * up_preactivation * slope_one
    up_gradient = hidden_gradient * act_gate
    tangent_gate_gradient = (
        tangent_hidden_gradient * up_preactivation * slope_one
        + hidden_gradient * tangent_up * slope_one
        + hidden_gradient * up_preactivation * slope_two * tangent_gate
    )
    tangent_up_gradient = (
        tangent_hidden_gradient * act_gate + hidden_gradient * slope_one * tangent_gate
    )
    blended_gate = adapter_scale * (
        gated_product(direction_gate_adapter, gate_gradient.T)
        + gated_product(adapter_gate_factor, tangent_gate_gradient.T)
    )
    blended_up = adapter_scale * (
        gated_product(direction_up_adapter, up_gradient.T)
        + gated_product(adapter_up_factor, tangent_up_gradient.T)
    )
    tangent_reduced_down = gated_product(adapter_down_factor, tangent_hidden.T) + gated_product(
        direction_down_adapter, hidden_state.T
    )
    blended_product = lax.psum(jnp.stack([blended_gate, blended_up, tangent_reduced_down]), "fsdp")
    local_tokens = tokens.astype(jnp.float32)
    local_cotangent = cotangent.astype(jnp.float32)
    part_model = jnp.stack(
        [
            gated_product(blended_product[0], local_tokens),
            gated_product(blended_product[1], local_tokens),
            adapter_scale * gated_product(blended_product[2], local_cotangent),
        ]
    )
    part_hidden = jnp.stack(
        [
            adapter_scale
            * (
                gated_product(tangent_projected_gate, gate_gradient)
                + gated_product(projected_gate, tangent_gate_gradient)
            ),
            adapter_scale
            * (
                gated_product(tangent_projected_up, up_gradient)
                + gated_product(projected_up, tangent_up_gradient)
            ),
            adapter_scale
            * (
                gated_product(tangent_projected_cotangent, hidden_state)
                + gated_product(projected_cotangent, tangent_hidden)
            ),
        ]
    )
    curvature_model, curvature_hidden = lax.psum((part_model, part_hidden), "grp")
    beta = beta_prev[0]
    along_local = jnp.sum(curvature_model * direction_model) + jnp.sum(
        curvature_hidden * direction_hidden
    )
    square_local = jnp.sum(direction_model * direction_model) + jnp.sum(
        direction_hidden * direction_hidden
    )
    along, square = lax.psum((along_local, square_local), "fsdp")
    alpha = along / square
    resid_model = curvature_model - alpha * direction_model - beta * previous_model
    resid_hidden = curvature_hidden - alpha * direction_hidden - beta * previous_hidden
    total = lax.psum(
        jnp.sum(resid_model * resid_model) + jnp.sum(resid_hidden * resid_hidden), "fsdp"
    )
    factor = lax.rsqrt(total / (R * (3 * D + 3 * FF)) + 1e-06)
    return (resid_model * factor, resid_hidden * factor, jnp.reshape(alpha, (1,)))


MESH = pl.DeviceIdType.MESH
NT = (((1,), (1,)), ((), ()))
NN = (((1,), (0,)), ((), ()))
CHIPS = 8
BLOCKS = 4
GROUPS = 6
TILE = 256


def mm(left, right, dims=NN):
    return lax.dot_general(left, right, dims, preferred_element_type=jnp.float32)


def high_low(value):
    high = value.astype(jnp.bfloat16)
    return high, (value - high.astype(jnp.float32)).astype(jnp.bfloat16)


def fused_kernel(
    tok,
    cot,
    w_gate,
    w_up,
    w_down,
    ad_m,
    ad_h,
    dir_m,
    dir_h,
    prev_m,
    prev_h,
    beta_ref,
    out_m,
    out_h,
    out_a,
    buf,
    acc,
    rbuf,
    wgu,
    wdn,
    pp,
    rsp,
    pall,
    prows,
    left,
    right,
    hid,
    mp,
    rsm,
    mall,
    st,
    h_m,
    h_h,
    own_sem,
    w_sem,
    sib_s,
    z_s,
    x_s,
    c_r,
    pr_s,
    pr_r,
    pg_s,
    pg_r,
    part_s,
    part_r,
    hid_s,
    hid_r,
    mr_s,
    mr_r,
    mg_s,
    mg_r,
    st_s,
    st_r,
):
    job = lax.axis_index("jobs")
    f = lax.axis_index("fsdp")
    g = lax.axis_index("grp")
    z = f // 2
    x = lax.rem(f, 2)
    o = 1 - g
    rows = buf.shape[2]
    depth = buf.shape[3]
    cols = acc.shape[3]
    home = (z // 2) == g
    away = jnp.logical_not(home)
    own = jnp.where(home, f - g * BLOCKS, BLOCKS)
    sib_own = jnp.where(home, BLOCKS, f - o * BLOCKS)
    near = jnp.where(home, z - 2 * g, 1 - g)
    far = 1 - near
    drains = []

    def send(src, dst, ss, rs, dev, pred=None):
        def make():
            return pltpu.make_async_remote_copy(
                src_ref=src, dst_ref=dst, send_sem=ss, recv_sem=rs, device_id=dev, device_id_type=MESH
            )

        if pred is None:
            make().start()
        else:
            pl.when(pred)(lambda: make().start())
        return make

    def drain(make, pred=None):
        drains.append((make, pred))

    def landed(ref, rs):
        pltpu.make_async_remote_copy(
            src_ref=ref, dst_ref=ref, send_sem=sib_s.at[0], recv_sem=rs, device_id=(job, f, o), device_id_type=MESH
        ).wait_recv()

    for a, src in enumerate((tok, cot)):
        pltpu.make_async_copy(src, buf.at[own, 2 * a + g], own_sem.at[a]).start()

    order = [near * 2 + x, near * 2 + 1 - x, far * 2 + x, far * 2 + 1 - x]

    def w_copy(piece):
        stage, kind = piece // 3, piece % 3
        at = pl.ds(pl.multiple_of(order[stage] * depth, depth), depth)
        if kind < 2:
            q = (2 * stage + kind) % 3
            return pltpu.make_async_copy((w_gate, w_up)[kind].at[at, :], wgu.at[q], w_sem.at[q])
        q = stage % 2
        return pltpu.make_async_copy(w_down.at[:, at], wdn.at[q], w_sem.at[3 + q])

    for piece in (0, 1, 2, 3, 5):
        w_copy(piece).start()

    barrier = pltpu.get_barrier_semaphore()
    for r in range(CHIPS):
        for t in range(2):

            @pl.when(jnp.logical_or(f != r, g != t))
            def _():
                pl.semaphore_signal(barrier, inc=1, device_id=(job, r, t), device_id_type=MESH)

    pl.semaphore_wait(barrier, 2 * CHIPS - 1)

    for a, src in enumerate((tok, cot)):
        drain(send(src, buf.at[sib_own, 2 * a + g], sib_s.at[a], c_r.at[sib_own, 2 * a + g], (job, f, o)))
    for a, src in enumerate((tok, cot)):
        pltpu.make_async_copy(src, buf.at[own, 2 * a + g], own_sem.at[a]).wait()

    def relay(i, k, c):
        zb = 2 * g + i
        slot = i * 2 + x
        ref = buf.at[slot, c]
        sem = c_r.at[slot, c]
        up = jnp.logical_and(z >= zb, z < 3)
        down = jnp.logical_and(z <= zb, z > 0)
        send(ref, ref, x_s.at[k, c], sem, (job, f + 1 - 2 * x, g))
        send(ref, ref, z_s.at[0, k, c], sem, (job, f + 2, g), up)
        send(ref, ref, z_s.at[1, k, c], sem, (job, f - 2, g), down)

    def relay_drain(i, k, c):
        zb = 2 * g + i
        slot = i * 2 + x
        ref = buf.at[slot, c]
        sem = c_r.at[slot, c]
        up = jnp.logical_and(z >= zb, z < 3)
        down = jnp.logical_and(z <= zb, z > 0)

        def make(ss, dev):
            return pltpu.make_async_remote_copy(
                src_ref=ref, dst_ref=ref, send_sem=ss, recv_sem=sem, device_id=dev, device_id_type=MESH
            )

        make(x_s.at[k, c], (job, f + 1 - 2 * x, g)).wait_send()

        @pl.when(up)
        def _():
            make(z_s.at[0, k, c], (job, f + 2, g)).wait_send()

        @pl.when(down)
        def _():
            make(z_s.at[1, k, c], (job, f - 2, g)).wait_send()

    @pl.when(home)
    def _():
        for a in range(2):
            relay(near, 0, 2 * a + g)
        for a in range(2):
            landed(buf.at[own, 2 * a + o], c_r.at[own, 2 * a + o])
            relay(near, 0, 2 * a + o)

    dir_b = dir_m[...].astype(jnp.bfloat16)
    low_t = jnp.concatenate([ad_m[:2], dir_b[:2]], 0).reshape(64, depth)
    low_c = jnp.concatenate([ad_m[2], dir_b[2]], 0)
    got_t = mm(low_t, buf[own, g], NT)
    got_c = mm(low_c, buf[own, 2 + g], NT)
    for k, v in enumerate(
        (got_t[0:16], got_t[16:32], got_c[0:16], got_t[32:48], got_t[48:64], got_c[16:32])
    ):
        pp[k] = v
    for r in range(GROUPS):
        other = f != r
        drain(send(pp.at[r], rsp.at[f], pr_s.at[r], pr_r.at[f], (job, r, g), other), other)

        @pl.when(f == r)
        def _():
            rsp[r] = pp[r]

    @pl.when(away)
    def _():
        for c in range(4):
            landed(buf.at[near * 2 + x, c], c_r.at[near * 2 + x, c])
            relay(near, 0, c)

    def product(kind, stage, half, first):
        q = (2 * stage + kind) % 3 if kind < 2 else stage % 2
        a = 0 if kind < 2 else 1
        slot = order[stage]

        def step(n, carry):
            at = pl.ds(pl.multiple_of(n * TILE, TILE), TILE)
            wat = pl.ds(pl.multiple_of(half * cols + n * TILE, TILE), TILE)
            value = buf[slot, 2 * a : 2 * a + 2].reshape(2 * rows, depth)
            if kind < 2:
                got = mm(value, wgu[q, :, wat])
            else:
                got = mm(value, wdn[q, wat, :], NT)
            if not first:
                got = acc[kind, half, :, at] + got
            acc[kind, half, :, at] = got
            return carry

        lax.fori_loop(0, cols // TILE, step, 0)

    def after(piece):
        kind, stage = piece % 3, piece // 3
        if kind < 2:
            nxt = 2 * stage + kind + 3
            if nxt < 8:
                w_copy((nxt // 2) * 3 + nxt % 2).start()
        elif stage + 2 < 4:
            w_copy((stage + 2) * 3 + 2).start()

    def compute(stage):
        for kind in range(3):
            w_copy(stage * 3 + kind).wait()
            for half in range(2):
                product(kind, stage, half, stage == 0)
            after(stage * 3 + kind)

    compute(0)
    for c in range(4):
        landed(buf.at[far * 2 + x, c], c_r.at[far * 2 + x, c])
        relay(far, 1, c)

    @pl.when(f < GROUPS)
    def _():
        for s in range(CHIPS):

            @pl.when(f != s)
            def _():
                landed(rsp.at[s], pr_r.at[s])

        pall[f, g] = jnp.sum(rsp[...], axis=0)

    for r in range(CHIPS):
        for t in range(2):
            pred = jnp.logical_and(f < GROUPS, jnp.logical_or(f != r, g != t))
            drain(
                send(pall.at[f, g], pall.at[f, g], pg_s.at[2 * r + t], pg_r.at[f, g], (job, r, t), pred), pred
            )

    for c in range(4):
        landed(buf.at[near * 2 + 1 - x, c], c_r.at[near * 2 + 1 - x, c])
    compute(1)
    compute(2)

    for r in range(GROUPS):
        for t in range(2):

            @pl.when(jnp.logical_or(f != r, g != t))
            def _():
                landed(pall.at[r, t], pg_r.at[r, t])

    for r in range(8):
        for t in range(2):
            at = slice(t * rows, (t + 1) * rows)
            if r < GROUPS:
                prows[16 * r : 16 * r + 16, at] = pall[r, t]
            else:
                prows[16 * r : 16 * r + 16, at] = jnp.zeros((16, rows), jnp.float32)
    turned = jnp.transpose(prows[...])
    t_high, t_low = high_low(turned)
    left[:, 0:128] = t_high
    left[:, 128:256] = t_low
    mine = pl.ds(pl.multiple_of(g * cols, cols), cols)
    right[...] = jnp.zeros(right.shape, right.dtype)
    for k in range(3):
        b = ad_h[k, :, mine] * jnp.bfloat16(2.0)
        v = dir_h[k, :, mine].astype(jnp.bfloat16) * jnp.bfloat16(2.0)
        for base in (0, 128):
            right[k, base + 16 * k : base + 16 * k + 16, :] = b
            right[3 + k, base + 48 + 16 * k : base + 64 + 16 * k, :] = b
            right[3 + k, base + 16 * k : base + 16 * k + 16, :] = v
    hid[g] = jnp.zeros(hid.shape[1:], jnp.float32)
    mp[...] = jnp.zeros(mp.shape, jnp.float32)
    p_high, p_low = high_low(prows[...])

    for c in range(4):
        landed(buf.at[far * 2 + 1 - x, c], c_r.at[far * 2 + 1 - x, c])
    for kind in range(3):
        w_copy(9 + kind).wait()
        product(kind, 3, o, False)
        drain(send(acc.at[kind, o], rbuf.at[kind], part_s.at[kind], part_r.at[kind], (job, f, o)))
    for kind in range(3):
        product(kind, 3, g, False)
    for kind in range(3):
        landed(rbuf.at[kind], part_r.at[kind])

    for t in range(2):
        rat = slice(t * rows, (t + 1) * rows)
        lft = left[rat, :]
        ph = p_high[:, rat]
        pw = p_low[:, rat]
        pairs = [
            (
                jnp.concatenate([ph[16 * k : 16 * k + 16], pw[16 * k : 16 * k + 16]], 0),
                jnp.concatenate([ph[48 + 16 * k : 64 + 16 * k], pw[48 + 16 * k : 64 + 16 * k]], 0),
            )
            for k in range(3)
        ]

        def step(n, carry, t=t, rat=rat, lft=lft, pairs=pairs):
            at = pl.ds(pl.multiple_of(n * TILE, TILE), TILE)
            hat = pl.ds(pl.multiple_of(g * cols + n * TILE, TILE), TILE)

            def base(k):
                return acc[k, g, rat, at] + rbuf[k, rat, at] + mm(lft, right[k, :, at])

            gate = base(0)
            up = base(1)
            grad = base(2)
            tan_gate = mm(lft, right[3, :, at])
            tan_up = mm(lft, right[4, :, at])
            tan_grad = mm(lft, right[5, :, at])
            sg = jax.nn.sigmoid(gate)
            act = gate * sg
            rest = 1.0 - sg
            one = sg * (1.0 + gate * rest)
            two = sg * rest * (2.0 + gate * (1.0 - 2.0 * sg))
            up_one = up * one
            one_tan = one * tan_gate
            values = (
                (grad * up_one, tan_grad * up_one + grad * (tan_up * one + up * (two * tan_gate))),
                (grad * act, tan_grad * act + grad * one_tan),
                (act * up, one_tan * up + act * tan_up),
            )
            for k in range(3):
                first, first_low = high_low(values[k][0])
                second, second_low = high_low(values[k][1])
                b = ad_h[k, :, hat]
                v = dir_h[k, :, hat].astype(jnp.bfloat16)
                part = (mm(v, first, NT) + mm(b, second, NT)) + (mm(v, first_low, NT) + mm(b, second_low, NT))
                mp[2 * k, t] += part[0:8]
                mp[2 * k + 1, t] += part[8:16]
                q = mm(pairs[k][1], first) + mm(pairs[k][0], second)
                w = mm(pairs[k][1][0:16], first_low) + mm(pairs[k][0][0:16], second_low)
                hid[g, k, :, at] += 2.0 * (q[0:16] + (q[16:32] + w))
            return carry

        lax.fori_loop(0, cols // TILE, step, 0)

    for r in range(GROUPS):
        for t in range(2):
            other = jnp.logical_or(f != r, g != t)
            drain(
                send(mp.at[r, t], rsm.at[f, g], mr_s.at[r, t], mr_r.at[f, g], (job, r, t), other), other
            )

            @pl.when(jnp.logical_not(other))
            def _():
                rsm[r, t] = mp[r, t]

    drain(send(hid.at[g], hid.at[g], hid_s.at[0], hid_r.at[0], (job, f, o)))

    @pl.when(f < GROUPS)
    def _():
        for r in range(CHIPS):
            for t in range(2):

                @pl.when(jnp.logical_or(f != r, g != t))
                def _():
                    landed(rsm.at[r, t], mr_r.at[r, t])

        mall[f, g] = jnp.sum(rsm[...].reshape(2 * CHIPS, 8, rows), axis=0)

    for r in range(CHIPS):
        for t in range(2):
            pred = jnp.logical_and(f < GROUPS, jnp.logical_or(f != r, g != t))
            drain(
                send(mall.at[f, g], mall.at[f, g], mg_s.at[2 * r + t], mg_r.at[f, g], (job, r, t), pred), pred
            )

    @pl.when(away)
    def _():
        for a in range(2):
            landed(buf.at[own, 2 * a + o], c_r.at[own, 2 * a + o])

    landed(hid.at[o], hid_r.at[0])
    beta = beta_ref[0]
    dh = dir_h[...]
    hh = jnp.concatenate([hid[0], hid[1]], axis=-1)
    hh2 = hh - beta * prev_h[...]
    dm = dir_m[...]

    for r in range(GROUPS):
        for t in range(2):

            @pl.when(jnp.logical_or(f != r, g != t))
            def _():
                landed(mall.at[r, t], mg_r.at[r, t])

    whole = jnp.concatenate(
        [jnp.concatenate([mall[r, 0], mall[r, 1]], axis=-1) for r in range(GROUPS)], axis=0
    )
    m_high, m_low = high_low(whole)
    own_t = buf[own, 0:2].reshape(2 * rows, depth)
    own_c = buf[own, 2:4].reshape(2 * rows, depth)
    res_t = mm(jnp.concatenate([m_high[0:32], m_low[0:32]], 0), own_t)
    res_c = mm(jnp.concatenate([m_high[32:48], m_low[32:48]], 0), own_c)
    hm = 2.0 * jnp.concatenate([res_t[0:32] + res_t[32:64], res_c[0:16] + res_c[16:32]], 0).reshape(
        3, 16, depth
    )
    hm2 = hm - beta * prev_m[...]

    def total(v, w):
        return jnp.sum(v) + jnp.sum(w)

    square = total(dm * dm, dh * dh)
    along = total(hm * dm, hh * dh)
    along2 = total(hm2 * dm, hh2 * dh)
    slope = jnp.where(square > 0.0, along2 / jnp.where(square > 0.0, square, 1.0), 0.0)
    em = hm2 - slope * dm
    eh = hh2 - slope * dh
    left_over = total(em * em, eh * eh)
    h_m[...] = hm2
    h_h[...] = hh2
    line = lax.broadcasted_iota(jnp.int32, (8, 128), 0)
    tile = jnp.where(
        line == 0, square, jnp.where(line == 1, along, jnp.where(line == 2, slope, left_over))
    )
    st[f] = tile
    for r in range(CHIPS):
        other = f != r
        drain(send(st.at[f], st.at[f], st_s.at[r], st_r.at[f], (job, r, g), other), other)
    for r in range(CHIPS):

        @pl.when(f != r)
        def _():
            landed(st.at[r], st_r.at[r])

    every = st[...]
    sq, al, sl, lo = (every[:, k, :] for k in range(4))
    alpha = jnp.sum(al, axis=0, keepdims=True) / jnp.sum(sq, axis=0, keepdims=True)
    away_sq = (alpha - sl) * (alpha - sl) * sq
    ms = jnp.sum(lo + away_sq, axis=0, keepdims=True) / float(R * (3 * D + 3 * FF))
    factor = lax.rsqrt(ms + 1e-06)
    out_a[...] = alpha
    one_alpha = alpha[0:1, 0:1].reshape(1, 1, 1)
    one_factor = factor[0:1, 0:1].reshape(1, 1, 1)
    out_m[...] = (h_m[...] - one_alpha * dir_m[...]) * one_factor
    out_h[...] = (h_h[...] - one_alpha * dir_h[...]) * one_factor

    for k, i in enumerate((near, far)):
        for c in range(4):
            relay_drain(i, k, c)
    for make, pred in drains:
        if pred is None:
            make().wait_send()
        else:
            pl.when(pred)(lambda make=make: make().wait_send())


def fused_body(tok, cot, w_gate, w_up, w_down, ad_m, ad_h, dir_m, dir_h, prev_m, prev_h, beta):
    rows, depth = tok.shape
    units = w_gate.shape[1]
    cols = units // 2
    bf, f32 = jnp.bfloat16, jnp.float32
    vmem = pl.BlockSpec(memory_space=pltpu.VMEM)
    hbm = pl.BlockSpec(memory_space=pl.ANY)
    dma = pltpu.SemaphoreType.DMA
    next_m, next_h, alpha = pl.pallas_call(
        fused_kernel,
        out_shape=(
            jax.ShapeDtypeStruct(dir_m.shape, f32),
            jax.ShapeDtypeStruct(dir_h.shape, f32),
            jax.ShapeDtypeStruct((1, 128), f32),
        ),
        in_specs=[hbm] * 5 + [vmem] * 6 + [pl.BlockSpec(memory_space=pltpu.SMEM)],
        out_specs=(vmem, vmem, vmem),
        scratch_shapes=[
            pltpu.VMEM((BLOCKS + 1, 4, rows, depth), bf),
            pltpu.VMEM((3, 2, 2 * rows, cols), f32),
            pltpu.VMEM((3, 2 * rows, cols), f32),
            pltpu.VMEM((3, depth, units), bf),
            pltpu.VMEM((2, units, depth), bf),
            pltpu.VMEM((GROUPS, 16, rows), f32),
            pltpu.VMEM((CHIPS, 16, rows), f32),
            pltpu.VMEM((GROUPS, 2, 16, rows), f32),
            pltpu.VMEM((128, 2 * rows), f32),
            pltpu.VMEM((2 * rows, 256), bf),
            pltpu.VMEM((6, 256, cols), bf),
            pltpu.VMEM((2, 3, 16, cols), f32),
            pltpu.VMEM((GROUPS, 2, 8, rows), f32),
            pltpu.VMEM((CHIPS, 2, 8, rows), f32),
            pltpu.VMEM((GROUPS, 2, 8, rows), f32),
            pltpu.VMEM((CHIPS, 8, 128), f32),
            pltpu.VMEM(dir_m.shape, f32),
            pltpu.VMEM(dir_h.shape, f32),
            dma((2,)),
            dma((5,)),
            dma((2,)),
            dma((2, 2, 4)),
            dma((2, 4)),
            dma((BLOCKS + 1, 4)),
            dma((GROUPS,)),
            dma((CHIPS,)),
            dma((2 * CHIPS,)),
            dma((GROUPS, 2)),
            dma((3,)),
            dma((3,)),
            dma((1,)),
            dma((1,)),
            dma((GROUPS, 2)),
            dma((CHIPS, 2)),
            dma((2 * CHIPS,)),
            dma((GROUPS, 2)),
            dma((CHIPS,)),
            dma((CHIPS,)),
        ],
        compiler_params=pltpu.CompilerParams(
            collective_id=0, has_side_effects=True, vmem_limit_bytes=62 * 1024 * 1024
        ),
        cost_estimate=pl.CostEstimate(
            flops=6 * 2 * rows * BLOCKS * depth * units,
            bytes_accessed=6 * BLOCKS * depth * units,
            transcendentals=2 * rows * cols,
        ),
    )(tok, cot, w_gate, w_up, w_down, ad_m, ad_h, dir_m, dir_h, prev_m, prev_h, beta)
    return next_m, next_h, alpha[0, :1]


def solution(mesh):
    placed = (
        P(("jobs", "grp"), "fsdp"),
        P(("jobs", "grp"), "fsdp"),
        P("grp", "fsdp"),
        P("grp", "fsdp"),
        P("fsdp", "grp"),
        P("jobs", None, "fsdp"),
        P("jobs", None, "fsdp"),
        P("jobs", None, "fsdp"),
        P("jobs", None, "fsdp"),
        P("jobs", None, "fsdp"),
        P("jobs", None, "fsdp"),
        P("jobs"),
    )
    chips = mesh.shape["fsdp"]
    use = fused_body if chips == 8 and mesh.shape["grp"] == 2 else body
    return jax.shard_map(
        use,
        mesh=mesh,
        in_specs=placed,
        out_specs=(P("jobs", None, "fsdp"), P("jobs", None, "fsdp"), P("jobs")),
        check_vma=False,
    )
```

```python
import functools
import jax
import jax.numpy as jnp
from jax import lax
from jax.experimental import pallas as pl
from jax.experimental.pallas import tpu as pltpu
from jax.sharding import PartitionSpec as P

D = 8192
FF = 16384
R = 16


adapter_scale = 2.0


def gated_product(left, right):
    return jnp.dot(left, right, precision=lax.Precision.HIGHEST, preferred_element_type=jnp.float32)


def lowrank_terms(adapt_part, dir_part, tok_part, cot_part):
    left_tok = jnp.concatenate([adapt_part[:2], dir_part[:2]], 0)
    left_cot = jnp.stack([adapt_part[2], dir_part[2]])
    low_tok = jnp.einsum("krn,tn->krt", left_tok, tok_part, preferred_element_type=jnp.float32)
    low_cot = jnp.einsum("krn,tn->krt", left_cot, cot_part, preferred_element_type=jnp.float32)
    return (low_tok, low_cot)


def body(
    tokens,
    cotangent,
    w_gate,
    w_up,
    w_down,
    adapt_model,
    adapt_hidden,
    direction_model,
    direction_hidden,
    previous_model,
    previous_hidden,
    beta_prev,
):
    dir_model = direction_model.astype(jnp.bfloat16)
    dir_hidden = direction_hidden.astype(jnp.bfloat16)
    full_gate, full_up = (
        lax.all_gather(w_gate, "grp", axis=0, tiled=True),
        lax.all_gather(w_up, "grp", axis=0, tiled=True),
    )
    full_down = lax.all_gather(w_down, "grp", axis=1, tiled=True)
    wide_adapt, wide_dir = (
        lax.all_gather(adapt_model, "fsdp", axis=2, tiled=True),
        lax.all_gather(dir_model, "fsdp", axis=2, tiled=True),
    )
    tok_full, cot_full = (
        lax.all_gather(tokens, "fsdp", axis=1, tiled=True),
        lax.all_gather(cotangent, "fsdp", axis=1, tiled=True),
    )
    gate_baseline = jnp.dot(tok_full, full_gate, preferred_element_type=jnp.float32)
    up_baseline = jnp.dot(tok_full, full_up, preferred_element_type=jnp.float32)
    backward_baseline = lax.dot_general(
        cot_full, full_down, (((1,), (1,)), ((), ())), preferred_element_type=jnp.float32
    )
    low_tok, low_cot = lowrank_terms(wide_adapt, wide_dir, tok_full, cot_full)
    projected_gate, projected_up, tangent_projected_gate, tangent_projected_up = (
        low_tok[0],
        low_tok[1],
        low_tok[2],
        low_tok[3],
    )
    projected_cotangent, tangent_projected_cotangent = (low_cot[0], low_cot[1])
    reduced_hidden = adapt_hidden.astype(jnp.float32)
    tan_hidden_dir = dir_hidden.astype(jnp.float32)
    adapter_gate_factor, adapter_up_factor, adapter_down_factor = (
        reduced_hidden[0],
        reduced_hidden[1],
        reduced_hidden[2],
    )
    direction_gate_adapter, direction_up_adapter, direction_down_adapter = (
        tan_hidden_dir[0],
        tan_hidden_dir[1],
        tan_hidden_dir[2],
    )
    gate_preactivation = gate_baseline + adapter_scale * gated_product(
        projected_gate.T, adapter_gate_factor
    )
    up_preactivation = up_baseline + adapter_scale * gated_product(
        projected_up.T, adapter_up_factor
    )
    tangent_gate = adapter_scale * (
        gated_product(tangent_projected_gate.T, adapter_gate_factor)
        + gated_product(projected_gate.T, direction_gate_adapter)
    )
    tangent_up = adapter_scale * (
        gated_product(tangent_projected_up.T, adapter_up_factor)
        + gated_product(projected_up.T, direction_up_adapter)
    )
    sig_gate = jax.nn.sigmoid(gate_preactivation)
    act_gate = gate_preactivation * sig_gate
    slope_one = sig_gate * (1.0 + gate_preactivation * (1.0 - sig_gate))
    slope_two = sig_gate * (1.0 - sig_gate) * (2.0 + gate_preactivation * (1.0 - 2.0 * sig_gate))
    hidden_state = act_gate * up_preactivation
    tangent_hidden = slope_one * tangent_gate * up_preactivation + act_gate * tangent_up
    hidden_gradient = backward_baseline + adapter_scale * gated_product(
        projected_cotangent.T, adapter_down_factor
    )
    tangent_hidden_gradient = adapter_scale * (
        gated_product(tangent_projected_cotangent.T, adapter_down_factor)
        + gated_product(projected_cotangent.T, direction_down_adapter)
    )
    gate_gradient = hidden_gradient * up_preactivation * slope_one
    up_gradient = hidden_gradient * act_gate
    tangent_gate_gradient = (
        tangent_hidden_gradient * up_preactivation * slope_one
        + hidden_gradient * tangent_up * slope_one
        + hidden_gradient * up_preactivation * slope_two * tangent_gate
    )
    tangent_up_gradient = (
        tangent_hidden_gradient * act_gate + hidden_gradient * slope_one * tangent_gate
    )
    blended_gate = adapter_scale * (
        gated_product(direction_gate_adapter, gate_gradient.T)
        + gated_product(adapter_gate_factor, tangent_gate_gradient.T)
    )
    blended_up = adapter_scale * (
        gated_product(direction_up_adapter, up_gradient.T)
        + gated_product(adapter_up_factor, tangent_up_gradient.T)
    )
    tangent_reduced_down = gated_product(adapter_down_factor, tangent_hidden.T) + gated_product(
        direction_down_adapter, hidden_state.T
    )
    blended_product = lax.psum(jnp.stack([blended_gate, blended_up, tangent_reduced_down]), "fsdp")
    local_tokens = tokens.astype(jnp.float32)
    local_cotangent = cotangent.astype(jnp.float32)
    part_model = jnp.stack(
        [
            gated_product(blended_product[0], local_tokens),
            gated_product(blended_product[1], local_tokens),
            adapter_scale * gated_product(blended_product[2], local_cotangent),
        ]
    )
    part_hidden = jnp.stack(
        [
            adapter_scale
            * (
                gated_product(tangent_projected_gate, gate_gradient)
                + gated_product(projected_gate, tangent_gate_gradient)
            ),
            adapter_scale
            * (
                gated_product(tangent_projected_up, up_gradient)
                + gated_product(projected_up, tangent_up_gradient)
            ),
            adapter_scale
            * (
                gated_product(tangent_projected_cotangent, hidden_state)
                + gated_product(projected_cotangent, tangent_hidden)
            ),
        ]
    )
    curvature_model, curvature_hidden = lax.psum((part_model, part_hidden), "grp")
    beta = beta_prev[0]
    along_local = jnp.sum(curvature_model * direction_model) + jnp.sum(
        curvature_hidden * direction_hidden
    )
    square_local = jnp.sum(direction_model * direction_model) + jnp.sum(
        direction_hidden * direction_hidden
    )
    along, square = lax.psum((along_local, square_local), "fsdp")
    alpha = along / square
    resid_model = curvature_model - alpha * direction_model - beta * previous_model
    resid_hidden = curvature_hidden - alpha * direction_hidden - beta * previous_hidden
    total = lax.psum(
        jnp.sum(resid_model * resid_model) + jnp.sum(resid_hidden * resid_hidden), "fsdp"
    )
    factor = lax.rsqrt(total / (R * (3 * D + 3 * FF)) + 1e-06)
    return (resid_model * factor, resid_hidden * factor, jnp.reshape(alpha, (1,)))


MESH = pl.DeviceIdType.MESH
NT = (((1,), (1,)), ((), ()))
NN = (((1,), (0,)), ((), ()))
CHIPS = 8
BLOCKS = 4
GROUPS = 6
TILE = 256


def mm(left, right, dims=NN):
    return lax.dot_general(left, right, dims, preferred_element_type=jnp.float32)


def high_low(value):
    high = value.astype(jnp.bfloat16)
    return high, (value - high.astype(jnp.float32)).astype(jnp.bfloat16)


def fused_kernel(
    tok,
    cot,
    w_gate,
    w_up,
    w_down,
    ad_m,
    ad_h,
    dir_m,
    dir_h,
    prev_m,
    prev_h,
    beta_ref,
    out_m,
    out_h,
    out_a,
    buf,
    acc,
    rbuf,
    wgu,
    wdn,
    pp,
    rsp,
    pall,
    prows,
    left,
    right,
    hid,
    mp,
    rsm,
    mall,
    st,
    h_m,
    h_h,
    own_sem,
    w_sem,
    sib_s,
    z_s,
    x_s,
    c_r,
    pr_s,
    pr_r,
    pg_s,
    pg_r,
    part_s,
    part_r,
    hid_s,
    hid_r,
    mr_s,
    mr_r,
    mg_s,
    mg_r,
    st_s,
    st_r,
):
    job = lax.axis_index("jobs")
    f = lax.axis_index("fsdp")
    g = lax.axis_index("grp")
    z = f // 2
    x = lax.rem(f, 2)
    o = 1 - g
    rows = buf.shape[2]
    depth = buf.shape[3]
    cols = acc.shape[3]
    home = (z // 2) == g
    away = jnp.logical_not(home)
    own = jnp.where(home, f - g * BLOCKS, BLOCKS)
    sib_own = jnp.where(home, BLOCKS, f - o * BLOCKS)
    near = jnp.where(home, z - 2 * g, 1 - g)
    far = 1 - near
    drains = []

    def send(src, dst, ss, rs, dev, pred=None):
        def make():
            return pltpu.make_async_remote_copy(
                src_ref=src, dst_ref=dst, send_sem=ss, recv_sem=rs, device_id=dev, device_id_type=MESH
            )

        if pred is None:
            make().start()
        else:
            pl.when(pred)(lambda: make().start())
        return make

    def drain(make, pred=None):
        drains.append((make, pred))

    def landed(ref, rs):
        pltpu.make_async_remote_copy(
            src_ref=ref, dst_ref=ref, send_sem=sib_s.at[0], recv_sem=rs, device_id=(job, f, o), device_id_type=MESH
        ).wait_recv()

    for a, src in enumerate((tok, cot)):
        pltpu.make_async_copy(src, buf.at[own, 2 * a + g], own_sem.at[a]).start()

    order = [near * 2 + x, near * 2 + 1 - x, far * 2 + x, far * 2 + 1 - x]

    def w_copy(piece):
        stage, kind = piece // 3, piece % 3
        at = pl.ds(pl.multiple_of(order[stage] * depth, depth), depth)
        if kind < 2:
            q = (2 * stage + kind) % 3
            return pltpu.make_async_copy((w_gate, w_up)[kind].at[at, :], wgu.at[q], w_sem.at[q])
        q = stage % 2
        return pltpu.make_async_copy(w_down.at[:, at], wdn.at[q], w_sem.at[3 + q])

    for piece in (0, 1, 2, 3, 5):
        w_copy(piece).start()

    barrier = pltpu.get_barrier_semaphore()
    for r in range(CHIPS):
        for t in range(2):

            @pl.when(jnp.logical_or(f != r, g != t))
            def _():
                pl.semaphore_signal(barrier, inc=1, device_id=(job, r, t), device_id_type=MESH)

    pl.semaphore_wait(barrier, 2 * CHIPS - 1)

    for a, src in enumerate((tok, cot)):
        drain(send(src, buf.at[sib_own, 2 * a + g], sib_s.at[a], c_r.at[sib_own, 2 * a + g], (job, f, o)))
    for a, src in enumerate((tok, cot)):
        pltpu.make_async_copy(src, buf.at[own, 2 * a + g], own_sem.at[a]).wait()

    def relay(i, k, c):
        zb = 2 * g + i
        slot = i * 2 + x
        ref = buf.at[slot, c]
        sem = c_r.at[slot, c]
        up = jnp.logical_and(z >= zb, z < 3)
        down = jnp.logical_and(z <= zb, z > 0)
        send(ref, ref, z_s.at[0, k, c], sem, (job, f + 2, g), up)
        send(ref, ref, z_s.at[1, k, c], sem, (job, f - 2, g), down)
        send(ref, ref, x_s.at[k, c], sem, (job, f + 1 - 2 * x, g))

    def relay_drain(i, k, c):
        zb = 2 * g + i
        slot = i * 2 + x
        ref = buf.at[slot, c]
        sem = c_r.at[slot, c]
        up = jnp.logical_and(z >= zb, z < 3)
        down = jnp.logical_and(z <= zb, z > 0)

        def make(ss, dev):
            return pltpu.make_async_remote_copy(
                src_ref=ref, dst_ref=ref, send_sem=ss, recv_sem=sem, device_id=dev, device_id_type=MESH
            )

        make(x_s.at[k, c], (job, f + 1 - 2 * x, g)).wait_send()

        @pl.when(up)
        def _():
            make(z_s.at[0, k, c], (job, f + 2, g)).wait_send()

        @pl.when(down)
        def _():
            make(z_s.at[1, k, c], (job, f - 2, g)).wait_send()

    @pl.when(home)
    def _():
        for a in range(2):
            relay(near, 0, 2 * a + g)
        for a in range(2):
            landed(buf.at[own, 2 * a + o], c_r.at[own, 2 * a + o])
            relay(near, 0, 2 * a + o)

    dir_b = dir_m[...].astype(jnp.bfloat16)
    low_t = jnp.concatenate([ad_m[:2], dir_b[:2]], 0).reshape(64, depth)
    low_c = jnp.concatenate([ad_m[2], dir_b[2]], 0)
    got_t = mm(low_t, buf[own, g], NT)
    got_c = mm(low_c, buf[own, 2 + g], NT)
    for k, v in enumerate(
        (got_t[0:16], got_t[16:32], got_c[0:16], got_t[32:48], got_t[48:64], got_c[16:32])
    ):
        pp[k] = v
    for r in range(GROUPS):
        other = f != r
        drain(send(pp.at[r], rsp.at[f], pr_s.at[r], pr_r.at[f], (job, r, g), other), other)

        @pl.when(f == r)
        def _():
            rsp[r] = pp[r]

    @pl.when(away)
    def _():
        for c in range(4):
            landed(buf.at[near * 2 + x, c], c_r.at[near * 2 + x, c])
            relay(near, 0, c)

    def product(kind, stage, half, first):
        q = (2 * stage + kind) % 3 if kind < 2 else stage % 2
        a = 0 if kind < 2 else 1
        slot = order[stage]

        def step(n, carry):
            at = pl.ds(pl.multiple_of(n * TILE, TILE), TILE)
            wat = pl.ds(pl.multiple_of(half * cols + n * TILE, TILE), TILE)
            value = buf[slot, 2 * a : 2 * a + 2].reshape(2 * rows, depth)
            if kind < 2:
                got = mm(value, wgu[q, :, wat])
            else:
                got = mm(value, wdn[q, wat, :], NT)
            if not first:
                got = acc[kind, half, :, at] + got
            acc[kind, half, :, at] = got
            return carry

        lax.fori_loop(0, cols // TILE, step, 0)

    def after(piece):
        kind, stage = piece % 3, piece // 3
        if kind < 2:
            nxt = 2 * stage + kind + 3
            if nxt < 8:
                w_copy((nxt // 2) * 3 + nxt % 2).start()
        elif stage + 2 < 4:
            w_copy((stage + 2) * 3 + 2).start()

    def compute(stage):
        for kind in range(3):
            w_copy(stage * 3 + kind).wait()
            for half in range(2):
                product(kind, stage, half, stage == 0)
            after(stage * 3 + kind)

    compute(0)
    for c in range(4):
        landed(buf.at[far * 2 + x, c], c_r.at[far * 2 + x, c])
        relay(far, 1, c)

    @pl.when(f < GROUPS)
    def _():
        for s in range(CHIPS):

            @pl.when(f != s)
            def _():
                landed(rsp.at[s], pr_r.at[s])

        pall[f, g] = jnp.sum(rsp[...], axis=0)

    for r in range(CHIPS):
        for t in range(2):
            pred = jnp.logical_and(f < GROUPS, jnp.logical_or(f != r, g != t))
            drain(
                send(pall.at[f, g], pall.at[f, g], pg_s.at[2 * r + t], pg_r.at[f, g], (job, r, t), pred), pred
            )

    for c in range(4):
        landed(buf.at[near * 2 + 1 - x, c], c_r.at[near * 2 + 1 - x, c])
    compute(1)
    compute(2)

    for r in range(GROUPS):
        for t in range(2):

            @pl.when(jnp.logical_or(f != r, g != t))
            def _():
                landed(pall.at[r, t], pg_r.at[r, t])

    for r in range(8):
        for t in range(2):
            at = slice(t * rows, (t + 1) * rows)
            if r < GROUPS:
                prows[16 * r : 16 * r + 16, at] = pall[r, t]
            else:
                prows[16 * r : 16 * r + 16, at] = jnp.zeros((16, rows), jnp.float32)
    turned = jnp.transpose(prows[...])
    t_high, t_low = high_low(turned)
    left[:, 0:128] = t_high
    left[:, 128:256] = t_low
    mine = pl.ds(pl.multiple_of(g * cols, cols), cols)
    right[...] = jnp.zeros(right.shape, right.dtype)
    for k in range(3):
        b = ad_h[k, :, mine] * jnp.bfloat16(2.0)
        v = dir_h[k, :, mine].astype(jnp.bfloat16) * jnp.bfloat16(2.0)
        for base in (0, 128):
            right[k, base + 16 * k : base + 16 * k + 16, :] = b
            right[3 + k, base + 48 + 16 * k : base + 64 + 16 * k, :] = b
            right[3 + k, base + 16 * k : base + 16 * k + 16, :] = v
    hid[g] = jnp.zeros(hid.shape[1:], jnp.float32)
    mp[...] = jnp.zeros(mp.shape, jnp.float32)
    p_high, p_low = high_low(prows[...])

    def last(kind):
        w_copy(9 + kind).wait()
        product(kind, 3, o, False)
        drain(send(acc.at[kind, o], rbuf.at[kind], part_s.at[kind], part_r.at[kind], (job, f, o)))

    for c in (0, 1):
        landed(buf.at[far * 2 + 1 - x, c], c_r.at[far * 2 + 1 - x, c])
    last(0)
    last(1)
    product(0, 3, g, False)
    product(1, 3, g, False)
    for c in (2, 3):
        landed(buf.at[far * 2 + 1 - x, c], c_r.at[far * 2 + 1 - x, c])
    last(2)
    product(2, 3, g, False)
    for kind in range(3):
        landed(rbuf.at[kind], part_r.at[kind])

    for t in range(2):
        rat = slice(t * rows, (t + 1) * rows)
        lft = left[rat, :]
        ph = p_high[:, rat]
        pw = p_low[:, rat]
        pairs = [
            (
                jnp.concatenate([ph[16 * k : 16 * k + 16], pw[16 * k : 16 * k + 16]], 0),
                jnp.concatenate([ph[48 + 16 * k : 64 + 16 * k], pw[48 + 16 * k : 64 + 16 * k]], 0),
            )
            for k in range(3)
        ]

        def step(n, carry, t=t, rat=rat, lft=lft, pairs=pairs):
            at = pl.ds(pl.multiple_of(n * TILE, TILE), TILE)
            hat = pl.ds(pl.multiple_of(g * cols + n * TILE, TILE), TILE)

            def base(k):
                return acc[k, g, rat, at] + rbuf[k, rat, at] + mm(lft, right[k, :, at])

            gate = base(0)
            up = base(1)
            grad = base(2)
            tan_gate = mm(lft, right[3, :, at])
            tan_up = mm(lft, right[4, :, at])
            tan_grad = mm(lft, right[5, :, at])
            sg = jax.nn.sigmoid(gate)
            act = gate * sg
            rest = 1.0 - sg
            one = sg * (1.0 + gate * rest)
            two = sg * rest * (2.0 + gate * (1.0 - 2.0 * sg))
            up_one = up * one
            one_tan = one * tan_gate
            values = (
                (grad * up_one, tan_grad * up_one + grad * (tan_up * one + up * (two * tan_gate))),
                (grad * act, tan_grad * act + grad * one_tan),
                (act * up, one_tan * up + act * tan_up),
            )
            for k in range(3):
                first, first_low = high_low(values[k][0])
                second, second_low = high_low(values[k][1])
                b = ad_h[k, :, hat]
                v = dir_h[k, :, hat].astype(jnp.bfloat16)
                part = (mm(v, first, NT) + mm(b, second, NT)) + (mm(v, first_low, NT) + mm(b, second_low, NT))
                mp[2 * k, t] += part[0:8]
                mp[2 * k + 1, t] += part[8:16]
                q = mm(pairs[k][1], first) + mm(pairs[k][0], second)
                w = mm(pairs[k][1][0:16], first_low) + mm(pairs[k][0][0:16], second_low)
                hid[g, k, :, at] += 2.0 * (q[0:16] + (q[16:32] + w))
            return carry

        lax.fori_loop(0, cols // TILE, step, 0)

    for r in range(GROUPS):
        for t in range(2):
            other = jnp.logical_or(f != r, g != t)
            drain(
                send(mp.at[r, t], rsm.at[f, g], mr_s.at[r, t], mr_r.at[f, g], (job, r, t), other), other
            )

            @pl.when(jnp.logical_not(other))
            def _():
                rsm[r, t] = mp[r, t]

    drain(send(hid.at[g], hid.at[g], hid_s.at[0], hid_r.at[0], (job, f, o)))

    @pl.when(f < GROUPS)
    def _():
        for r in range(CHIPS):
            for t in range(2):

                @pl.when(jnp.logical_or(f != r, g != t))
                def _():
                    landed(rsm.at[r, t], mr_r.at[r, t])

        mall[f, g] = jnp.sum(rsm[...].reshape(2 * CHIPS, 8, rows), axis=0)

    for r in range(CHIPS):
        for t in range(2):
            pred = jnp.logical_and(f < GROUPS, jnp.logical_or(f != r, g != t))
            drain(
                send(mall.at[f, g], mall.at[f, g], mg_s.at[2 * r + t], mg_r.at[f, g], (job, r, t), pred), pred
            )

    @pl.when(away)
    def _():
        for a in range(2):
            landed(buf.at[own, 2 * a + o], c_r.at[own, 2 * a + o])

    landed(hid.at[o], hid_r.at[0])
    beta = beta_ref[0]
    dh = dir_h[...]
    hh = jnp.concatenate([hid[0], hid[1]], axis=-1)
    hh2 = hh - beta * prev_h[...]
    dm = dir_m[...]

    for r in range(GROUPS):
        for t in range(2):

            @pl.when(jnp.logical_or(f != r, g != t))
            def _():
                landed(mall.at[r, t], mg_r.at[r, t])

    whole = jnp.concatenate(
        [jnp.concatenate([mall[r, 0], mall[r, 1]], axis=-1) for r in range(GROUPS)], axis=0
    )
    m_high, m_low = high_low(whole)
    own_t = buf[own, 0:2].reshape(2 * rows, depth)
    own_c = buf[own, 2:4].reshape(2 * rows, depth)
    res_t = mm(jnp.concatenate([m_high[0:32], m_low[0:32]], 0), own_t)
    res_c = mm(jnp.concatenate([m_high[32:48], m_low[32:48]], 0), own_c)
    hm = 2.0 * jnp.concatenate([res_t[0:32] + res_t[32:64], res_c[0:16] + res_c[16:32]], 0).reshape(
        3, 16, depth
    )
    hm2 = hm - beta * prev_m[...]

    def total(v, w):
        return jnp.sum(v) + jnp.sum(w)

    square = total(dm * dm, dh * dh)
    along = total(hm * dm, hh * dh)
    along2 = total(hm2 * dm, hh2 * dh)
    slope = jnp.where(square > 0.0, along2 / jnp.where(square > 0.0, square, 1.0), 0.0)
    em = hm2 - slope * dm
    eh = hh2 - slope * dh
    left_over = total(em * em, eh * eh)
    h_m[...] = hm2
    h_h[...] = hh2
    line = lax.broadcasted_iota(jnp.int32, (8, 128), 0)
    tile = jnp.where(
        line == 0, square, jnp.where(line == 1, along, jnp.where(line == 2, slope, left_over))
    )
    st[f] = tile
    for r in range(CHIPS):
        other = f != r
        drain(send(st.at[f], st.at[f], st_s.at[r], st_r.at[f], (job, r, g), other), other)
    for r in range(CHIPS):

        @pl.when(f != r)
        def _():
            landed(st.at[r], st_r.at[r])

    every = st[...]
    sq, al, sl, lo = (every[:, k, :] for k in range(4))
    alpha = jnp.sum(al, axis=0, keepdims=True) / jnp.sum(sq, axis=0, keepdims=True)
    away_sq = (alpha - sl) * (alpha - sl) * sq
    ms = jnp.sum(lo + away_sq, axis=0, keepdims=True) / float(R * (3 * D + 3 * FF))
    factor = lax.rsqrt(ms + 1e-06)
    out_a[...] = alpha
    one_alpha = alpha[0:1, 0:1].reshape(1, 1, 1)
    one_factor = factor[0:1, 0:1].reshape(1, 1, 1)
    out_m[...] = (h_m[...] - one_alpha * dir_m[...]) * one_factor
    out_h[...] = (h_h[...] - one_alpha * dir_h[...]) * one_factor

    for k, i in enumerate((near, far)):
        for c in range(4):
            relay_drain(i, k, c)
    for make, pred in drains:
        if pred is None:
            make().wait_send()
        else:
            pl.when(pred)(lambda make=make: make().wait_send())


def fused_body(tok, cot, w_gate, w_up, w_down, ad_m, ad_h, dir_m, dir_h, prev_m, prev_h, beta):
    rows, depth = tok.shape
    units = w_gate.shape[1]
    cols = units // 2
    bf, f32 = jnp.bfloat16, jnp.float32
    vmem = pl.BlockSpec(memory_space=pltpu.VMEM)
    hbm = pl.BlockSpec(memory_space=pl.ANY)
    dma = pltpu.SemaphoreType.DMA
    next_m, next_h, alpha = pl.pallas_call(
        fused_kernel,
        out_shape=(
            jax.ShapeDtypeStruct(dir_m.shape, f32),
            jax.ShapeDtypeStruct(dir_h.shape, f32),
            jax.ShapeDtypeStruct((1, 128), f32),
        ),
        in_specs=[hbm] * 5 + [vmem] * 6 + [pl.BlockSpec(memory_space=pltpu.SMEM)],
        out_specs=(vmem, vmem, vmem),
        scratch_shapes=[
            pltpu.VMEM((BLOCKS + 1, 4, rows, depth), bf),
            pltpu.VMEM((3, 2, 2 * rows, cols), f32),
            pltpu.VMEM((3, 2 * rows, cols), f32),
            pltpu.VMEM((3, depth, units), bf),
            pltpu.VMEM((2, units, depth), bf),
            pltpu.VMEM((GROUPS, 16, rows), f32),
            pltpu.VMEM((CHIPS, 16, rows), f32),
            pltpu.VMEM((GROUPS, 2, 16, rows), f32),
            pltpu.VMEM((128, 2 * rows), f32),
            pltpu.VMEM((2 * rows, 256), bf),
            pltpu.VMEM((6, 256, cols), bf),
            pltpu.VMEM((2, 3, 16, cols), f32),
            pltpu.VMEM((GROUPS, 2, 8, rows), f32),
            pltpu.VMEM((CHIPS, 2, 8, rows), f32),
            pltpu.VMEM((GROUPS, 2, 8, rows), f32),
            pltpu.VMEM((CHIPS, 8, 128), f32),
            pltpu.VMEM(dir_m.shape, f32),
            pltpu.VMEM(dir_h.shape, f32),
            dma((2,)),
            dma((5,)),
            dma((2,)),
            dma((2, 2, 4)),
            dma((2, 4)),
            dma((BLOCKS + 1, 4)),
            dma((GROUPS,)),
            dma((CHIPS,)),
            dma((2 * CHIPS,)),
            dma((GROUPS, 2)),
            dma((3,)),
            dma((3,)),
            dma((1,)),
            dma((1,)),
            dma((GROUPS, 2)),
            dma((CHIPS, 2)),
            dma((2 * CHIPS,)),
            dma((GROUPS, 2)),
            dma((CHIPS,)),
            dma((CHIPS,)),
        ],
        compiler_params=pltpu.CompilerParams(
            collective_id=0, has_side_effects=True, vmem_limit_bytes=62 * 1024 * 1024
        ),
        cost_estimate=pl.CostEstimate(
            flops=6 * 2 * rows * BLOCKS * depth * units,
            bytes_accessed=6 * BLOCKS * depth * units,
            transcendentals=2 * rows * cols,
        ),
    )(tok, cot, w_gate, w_up, w_down, ad_m, ad_h, dir_m, dir_h, prev_m, prev_h, beta)
    return next_m, next_h, alpha[0, :1]


def solution(mesh):
    placed = (
        P(("jobs", "grp"), "fsdp"),
        P(("jobs", "grp"), "fsdp"),
        P("grp", "fsdp"),
        P("grp", "fsdp"),
        P("fsdp", "grp"),
        P("jobs", None, "fsdp"),
        P("jobs", None, "fsdp"),
        P("jobs", None, "fsdp"),
        P("jobs", None, "fsdp"),
        P("jobs", None, "fsdp"),
        P("jobs", None, "fsdp"),
        P("jobs"),
    )
    chips = mesh.shape["fsdp"]
    use = fused_body if chips == 8 and mesh.shape["grp"] == 2 else body
    return jax.shard_map(
        use,
        mesh=mesh,
        in_specs=placed,
        out_specs=(P("jobs", None, "fsdp"), P("jobs", None, "fsdp"), P("jobs")),
        check_vma=False,
    )
```
